256 devices in a mesh: grp: 8 (over x, core), sp: 32 (over z, y).
Axes of the slice: x: 4, y: 4, z: 8, core: 2. Of those that a mesh axis runs over, the one named last changes fastest.
Arguments:
- queries: bfloat16 [32768, 4096], P(('grp', 'sp')), may hold values from -36 to 36
- key_rows: bfloat16 [32768, 512], P(('grp', 'sp')), may hold values from -4 to 4
- value_rows: bfloat16 [32768, 512], P(('grp', 'sp')), may hold values from -6 to 6
- out_grad: bfloat16 [32768, 4096], P(('grp', 'sp')), may hold values from -6 to 6
- dest_group: int32 [32768, 1], P(('grp', 'sp')), may hold values from 0 to 7; in each aligned block of 128 rows (0 to 127, 128 to 255, ...) at most 18 rows name the same one
- slot_segment: int32 [8, 4608], P('grp', 'sp'), may hold values from 0 to 3, never falling along the last dimension, each value on 1 to 2048 neighbouring positions
Outputs:
- attn_out: bfloat16 [32768, 4096], P(('grp', 'sp'))
- grad_query: bfloat16 [32768, 4096], P(('grp', 'sp'))
- grad_key: bfloat16 [32768, 512], P(('grp', 'sp'))
- grad_value: bfloat16 [32768, 512], P(('grp', 'sp'))
The draws below stay inside these ranges and needn't reach their ends.
Inputs may be any that keep to these rules, and one draw needn't show every extreme that they name: `dest_group`: each loader device sends at most 18 of its rows to one group, and some device sends exactly 18 rows to some group. `slot_segment`: along the slots of a group the labels never fall; a run of equal labels spans 1 to 2048 slots, and some run spans exactly 2048.
All inputs are finite; a program needn't handle non-finite values.
Results may differ from the reference program's by a relative error of at most 0.015.
Values may be sent and summed in bfloat16 or wider, within the bound.
No kernel may reach another device: no remote copies, remote signals or barrier semaphores. Data moves between devices by JAX's collectives and lax.ppermute only.
A program may use at most 128 MiB of HBM per device.

```python
import math
import jax
import jax.numpy as jnp
import numpy as np
from jax import lax

H = 32
KV = 4
HD = 128
TOK_DEV = 128
QBLOCK = 128
LMAX = 2048
TOKENS = 32768
CAP = 18
SLOTS_DEV = 144
GSLOTS = 4608
SEQS = 4
N_GRP = 8
N_SP = 32


def shared_rows(key):
    rough = jax.random.normal(key, (TOKENS, KV * HD), jnp.float32)
    return rough


def draw_key_rows(key, part):
    rough = shared_rows(key)
    return jnp.clip(rough, -4.0, 4.0).astype(jnp.bfloat16)


def draw_queries(key, part):
    key = jax.random.fold_in(key, 5)
    return jnp.clip(jax.random.normal(key, (TOKENS, H * HD), jnp.float32), -4.0, 4.0).astype(jnp.bfloat16)


def level_of(rng, dims, shards, least, high):
    factor_of, own = 1.0, jax.random.fold_in(rng, 6)
    for dim, parts in shards:
        draws = jnp.exp(jax.random.uniform(jax.random.fold_in(own, dim), (parts,), jnp.float32, least / len(shards), high / len(shards)))
        factor_of = factor_of * jnp.repeat(draws, dims[dim] // parts).reshape([-1 if axis == dim else 1 for axis in range(len(dims))])
    return factor_of


def profile(number_of, total, bound, slope):
    weights = [(1 << 20) // math.isqrt(rank ** slope) + 1 for rank in range(2, number_of + 1)]
    surplus, counts = total - bound - (number_of - 1), [1] * (number_of - 1)
    while surplus > 0:
        candidates = [i for i in range(number_of - 1) if counts[i] < bound]
        pool, remaining = sum([weights[i] for i in candidates]), surplus
        for i in candidates:
            more = min(bound - counts[i], max(1, remaining * weights[i] // pool), surplus)
            counts[i] = counts[i] + more
            surplus = surplus - more
    return np.array([bound] + counts)


def ragged_sizes(own_key, number_of, total, reach, skew):
    if number_of == 2:
        one = jax.random.randint(own_key, (), max(1, total - reach), min(reach, total - 1) + 1)
        return jnp.stack([one, total - one])
    sizes = jnp.asarray(profile(number_of, total, reach, skew), jnp.int32)
    pairs = (number_of - 1) // 2
    donor, receiver = sizes[1:1 + 2 * pairs:2], sizes[2:2 + 2 * pairs:2]
    margin = jnp.minimum(donor - 1, reach - receiver)
    moved = jax.random.randint(jax.random.fold_in(own_key, 1), (pairs,), 0, 1 << 20) % (margin + 1)
    sizes = sizes.at[1:1 + 2 * pairs:2].set(donor - moved).at[2:2 + 2 * pairs:2].set(receiver + moved)
    return sizes[jax.random.permutation(jax.random.fold_in(own_key, 2), number_of)]


def routed_block(key, own, number, rows, amount, top, reach, slope):
    ranking = jax.random.permutation(key, amount)
    packed, ordinary = load_shares(amount, rows * top, reach, slope, True), load_shares(amount, rows * top, reach, slope, False)
    places = jnp.arange(amount)

    def named(tallies, rotation):
        used = int((tallies > 0).sum())
        fixed = max(1, used // 4)
        moved = fixed + (places - fixed + rotation * (used - fixed)) % max(1, amount - fixed)
        return jnp.zeros((amount,), jnp.int32).at[ranking[jnp.where(places < fixed, places, moved)]].set(jnp.asarray(tallies, jnp.int32))

    tallies = jnp.where(number % 4 == 0, named(packed, number // 4), named(ordinary, number - number // 4 - 1))
    mixed = jax.random.permutation(jax.random.fold_in(own, 3), amount)
    giver, taker = mixed[0:amount // 2 * 2:2], mixed[1:amount // 2 * 2:2]
    slack = jnp.minimum(tallies[giver] - 1, reach - tallies[taker]) // 2
    slack = jnp.where((giver == ranking[0]) | (taker == ranking[0]) | (tallies[taker] == 0), 0, jnp.maximum(slack, 0))
    moved = jax.random.randint(jax.random.fold_in(own, 4), (amount // 2,), 0, 1 << 20) % (slack + 1)
    tallies = tallies.at[giver].add(-moved).at[taker].add(moved)
    items = jnp.searchsorted(jnp.cumsum(tallies), jnp.arange(rows * top), side="right").astype(jnp.int32)
    grid = items.reshape(top, rows).T
    grid = grid[jax.random.permutation(jax.random.fold_in(own, 1), rows)]
    rotation = jax.random.randint(jax.random.fold_in(own, 2), (rows, 1), 0, top)
    return jnp.take_along_axis(grid, (jnp.arange(top)[None, :] + rotation) % top, axis=1)


def load_shares(count, total, most, lean, full):
    loads = [(1 << 20) // math.isqrt(rank ** lean) + 1 for rank in range(1, count + 1)]
    largest = most if full else min(most, max(-(-total // count), total * loads[0] // sum(loads)))
    least = 1 if total - largest >= count - 1 else 0
    given, spare = [largest] + [least] * (count - 1), total - largest - least * (count - 1)
    while spare > 0:
        free = [i for i in range(1, count) if given[i] < largest] or [i for i in range(1, count) if given[i] < most]
        pool, budget = sum([loads[i] for i in free]), spare
        for i in free:
            addition = min(most - given[i], max(1, budget * loads[i] // pool), spare)
            given[i] = given[i] + addition
            spare = spare - addition
    return np.array(given)


def centred(key, dims, scale, reach, cuts=(), kind=jnp.bfloat16):
    drawn = jax.random.normal(key, dims, jnp.float32) * scale
    if len(cuts) > 0:
        drawn = level_of(key, dims, cuts, -0.22, 0.18) * drawn
    return jnp.clip(drawn, min=-reach, max=reach).astype(kind)


def setup_inputs(seed: int = 0) -> dict:
    key_list = jax.random.split(jax.random.key(seed), 7)
    queries = draw_queries(jax.random.fold_in(key_list[6], 71), 0)
    key_rows = draw_key_rows(jax.random.fold_in(key_list[6], 71), 0)
    value_rows = centred(key_list[2], (TOKENS, KV * HD), 1.0, 6.0, ((0, 256),))
    out_grad = centred(key_list[3], (TOKENS, H * HD), 1.0, 6.0, ((0, 256),))
    dest_group_keys = jax.random.split(jax.random.fold_in(key_list[4], 1), TOKENS // TOK_DEV)
    dest_group_turns = jax.random.permutation(jax.random.fold_in(key_list[4], 3), TOKENS // TOK_DEV)
    dest_group = jax.vmap(lambda own, number: routed_block(jax.random.fold_in(key_list[4], 2), own, number, TOK_DEV, N_GRP, 1, CAP, 2))(dest_group_keys, dest_group_turns).reshape((TOKENS, 1))
    slot_segment = jax.vmap(lambda own: jnp.searchsorted(jnp.cumsum(ragged_sizes(own, SEQS, GSLOTS, LMAX, 2)), jnp.arange(GSLOTS), side="right"))(jax.random.split(key_list[5], N_GRP)).reshape((N_GRP, GSLOTS)).astype(jnp.int32)
    return {"queries": queries, "key_rows": key_rows, "value_rows": value_rows, "out_grad": out_grad, "dest_group": dest_group, "slot_segment": slot_segment}


def attend_block(query_blk, key_win, value_win, grad_blk, label_query, label_key, query_pos, key_pos):
    scaling = 1.0 / math.sqrt(query_blk.shape[-1])
    query_f = query_blk.astype(jnp.float32)
    key_f = key_win.astype(jnp.float32)
    value_f = value_win.astype(jnp.float32)
    grad_f = grad_blk.astype(jnp.float32)
    scores = jnp.einsum('qkgd,ckd->kgqc', query_f, key_f) * scaling
    allowed = (label_query[:, None] == label_key[None, :]) & (label_key[None, :] >= 0) & (key_pos[None, :] <= query_pos[:, None]) | (key_pos[None, :] == query_pos[:, None])
    scores = jnp.where(allowed, scores, -jnp.inf)
    row_max = lax.optimization_barrier(jnp.max(scores, axis=-1, keepdims=True))
    exponent = jnp.exp(scores - row_max)
    weights = exponent / lax.optimization_barrier(jnp.sum(exponent, axis=-1, keepdims=True))
    weights_b = lax.optimization_barrier(weights.astype(jnp.bfloat16))
    weights_f = weights_b.astype(jnp.float32)
    output = lax.optimization_barrier(jnp.einsum('kgqc,ckd->qkgd', weights_f, value_f).astype(jnp.bfloat16))
    row_delta = lax.optimization_barrier(jnp.sum(grad_f * output.astype(jnp.float32), axis=-1))
    dprod = jnp.einsum('qkgd,ckd->kgqc', grad_f, value_f)
    dscore = (weights * (dprod - jnp.transpose(row_delta, (1, 2, 0))[..., None])).astype(jnp.bfloat16)
    dscore_f = lax.optimization_barrier(dscore).astype(jnp.float32)
    grad_query = (jnp.einsum('kgqc,ckd->qkgd', dscore_f, key_f) * scaling).astype(jnp.bfloat16)
    grad_key = jnp.einsum('kgqc,qkgd->ckd', dscore_f, query_f) * scaling
    grad_value = jnp.einsum('kgqc,qkgd->ckd', weights_f, grad_f)
    return (output, grad_query, grad_key, grad_value)

def group_pass(pieces):
    query_g, key_g, value_g, grad_g, label_g = pieces
    grouped = H // KV
    width = QBLOCK + LMAX
    query_all = query_g.reshape(GSLOTS, KV, grouped, HD)
    grad_all = grad_g.reshape(GSLOTS, KV, grouped, HD)
    key_pad = jnp.concatenate([jnp.zeros((LMAX, KV, HD), key_g.dtype), key_g.reshape(GSLOTS, KV, HD)], axis=0)
    value_pad = jnp.concatenate([jnp.zeros((LMAX, KV, HD), value_g.dtype), value_g.reshape(GSLOTS, KV, HD)], axis=0)
    label_pad = jnp.concatenate([jnp.full((LMAX,), -1, jnp.int32), label_g], axis=0)

    def step(totals, block_index):
        key_acc, value_acc = totals
        offset = (block_index * QBLOCK).astype(jnp.int32)
        query_blk = lax.dynamic_slice_in_dim(query_all, offset, QBLOCK, 0)
        grad_blk = lax.dynamic_slice_in_dim(grad_all, offset, QBLOCK, 0)
        key_win = lax.dynamic_slice_in_dim(key_pad, offset, width, 0)
        value_win = lax.dynamic_slice_in_dim(value_pad, offset, width, 0)
        label_query = lax.dynamic_slice_in_dim(label_g, offset, QBLOCK, 0)
        label_key = lax.dynamic_slice_in_dim(label_pad, offset, width, 0)
        query_pos = offset + jnp.arange(QBLOCK, dtype=jnp.int32)
        key_pos = offset - LMAX + jnp.arange(width, dtype=jnp.int32)
        output, grad_query, grad_key, grad_value = attend_block(query_blk, key_win, value_win, grad_blk, label_query, label_key, query_pos, key_pos)
        key_acc = lax.dynamic_update_slice_in_dim(key_acc, lax.dynamic_slice_in_dim(key_acc, offset, width, 0) + grad_key, offset, 0)
        value_acc = lax.dynamic_update_slice_in_dim(value_acc, lax.dynamic_slice_in_dim(value_acc, offset, width, 0) + grad_value, offset, 0)
        return ((key_acc, value_acc), (output, grad_query))
    zeros = jnp.zeros((LMAX + GSLOTS, KV, HD), jnp.float32)
    (key_acc, value_acc), (outputs, grad_queries) = lax.scan(step, (zeros, zeros), jnp.arange(GSLOTS // QBLOCK, dtype=jnp.int32))
    return (outputs.reshape(GSLOTS, H * HD), grad_queries.reshape(GSLOTS, H * HD), key_acc[LMAX:].astype(jnp.bfloat16).reshape(GSLOTS, KV * HD), value_acc[LMAX:].astype(jnp.bfloat16).reshape(GSLOTS, KV * HD))

def reference(queries, key_rows, value_rows, out_grad, dest_group, slot_segment):
    devices_all = N_GRP * N_SP
    target_group = dest_group[:, 0].astype(jnp.int32)
    onehot = (target_group[:, None] == jnp.arange(N_GRP, dtype=jnp.int32)[None, :]).astype(jnp.int32)
    counted = jnp.cumsum(onehot.reshape(devices_all, TOK_DEV, N_GRP), axis=1, dtype=jnp.int32).reshape(TOKENS, N_GRP)
    rank_in = lax.optimization_barrier(jnp.sum((counted - 1) * onehot, axis=1, dtype=jnp.int32))
    device = jnp.arange(TOKENS, dtype=jnp.int32) // TOK_DEV
    position = device % N_SP * SLOTS_DEV + device // N_SP * CAP + rank_in
    flat_slot = (target_group * GSLOTS + position).astype(jnp.int32)

    def settle(matrix):
        empty = jnp.zeros((N_GRP * GSLOTS, matrix.shape[1]), matrix.dtype)
        return empty.at[flat_slot].set(matrix).reshape(N_GRP, GSLOTS, matrix.shape[1])
    occupied = jnp.zeros((N_GRP * GSLOTS,), jnp.int32).at[flat_slot].set(1).reshape(N_GRP, GSLOTS)
    labels = jnp.where(occupied > 0, slot_segment, -1).astype(jnp.int32)
    results = lax.map(group_pass, (settle(queries), settle(key_rows), settle(value_rows), settle(out_grad), labels))
    return (results[0].reshape(N_GRP * GSLOTS, H * HD)[flat_slot], results[1].reshape(N_GRP * GSLOTS, H * HD)[flat_slot], results[2].reshape(N_GRP * GSLOTS, KV * HD)[flat_slot], results[3].reshape(N_GRP * GSLOTS, KV * HD)[flat_slot])
```

```python
import math

import jax
import jax.numpy as jnp
from jax import lax
from jax.experimental import pallas as pl
from jax.experimental.pallas import tpu as pltpu
from jax.sharding import Mesh
from jax.sharding import PartitionSpec as P

H = 32
KV = 4
HD = 128
GH = H // KV
NG = 8
NZ = 8
NY = 4
CAP = 18
MAIN = 16
SUB = 144
PAIR = 288
CHUNK = 576
BACK = 4
PAIRS = 2 * (BACK + 1)
TILE = 256
TILES = 18
BIG = 2.0**24
EMPTY_KEY = 64.0
SCALE = 1.0 / math.sqrt(HD)
LOG2E = 1.4426950408889634
GY = ("grp", "y")
BF = jnp.bfloat16
F32 = jnp.float32
NN = (((1,), (0,)), ((), ()))
NT = (((1,), (1,)), ((), ()))
TN = (((0,), (0,)), ((), ()))
VM = 56 * 1024 * 1024


def dot(a, b, dims=NN):
    return lax.dot_general(a, b, dims, preferred_element_type=F32)


def iota(shape, dim):
    return lax.broadcasted_iota(jnp.int32, shape, dim)


def ranks(dest):
    onehot = (dest == iota((128, 128), 1)).astype(F32)
    earlier = (iota((128, 128), 1) < iota((128, 128), 0)).astype(BF)
    counted = dot(earlier, onehot.astype(BF))
    return jnp.sum(counted * onehot, axis=1, keepdims=True).astype(jnp.int32)


def placing(dest):
    rank = ranks(dest)
    main_at = jnp.where(rank < MAIN, dest * MAIN + rank, -1)
    tail_at = jnp.where(rank >= MAIN, dest * 2 + rank - MAIN, -1)
    slots = iota((128, 128), 1)
    main = (slots == main_at).astype(F32).T
    tail = (slots == tail_at).astype(F32).T[:16]
    return main, tail


def tail_perm(by_slice):
    rows, cols = iota((256, 256), 0), iota((256, 256), 1)
    if by_slice:
        want = ((rows % 16) // 2) * 32 + (rows // 16) * 2 + rows % 2
    else:
        want = ((rows % 32) // 2) * 16 + (rows // 32) * 2 + rows % 2
    return (cols == want).astype(BF)


def settle_kv_kernel(grp_ref, dest_ref, key_ref, value_ref, seg_ref, msg_ref):
    main, tail = placing(dest_ref[...])
    main_b, tail_b = main.astype(BF), tail.astype(BF)
    empty_main = (1.0 - jnp.sum(main, axis=1, keepdims=True)) * EMPTY_KEY
    empty_tail = (1.0 - jnp.sum(tail, axis=1, keepdims=True)) * EMPTY_KEY
    key_main = (dot(main_b, key_ref[...]) + empty_main).astype(BF)
    key_tail = (dot(tail_b, key_ref[...]) + empty_tail).astype(BF)
    value_main = dot(main_b, value_ref[...]).astype(BF)
    value_tail = dot(tail_b, value_ref[...]).astype(BF)
    seg = seg_ref[...]
    lane = iota((1, 128), 1)
    meta = jnp.zeros((1, 128), F32)
    for c in range(3):
        below = jnp.sum((seg <= c).astype(F32), axis=1, keepdims=True)
        meta = jnp.where(lane == c, below, meta)
    meta = jnp.broadcast_to(meta, (16, 128)).astype(BF)
    rows, cols = iota((128, 128), 0), iota((128, 128), 1)
    owner, item = rows // 16, rows % 16
    want = jnp.where(item < 2, owner * 2 + item, 16 + owner * 2 + item - 2)
    want = jnp.where(item < 4, want, jnp.where((item == 4) & (owner == grp_ref[0]), 32, -1))
    collect = (cols == want).astype(BF)
    blank = jnp.zeros((80, 128), BF)
    for y in range(NY):
        lanes = slice(y * HD, (y + 1) * HD)
        stacked = jnp.concatenate([key_tail[:, lanes], value_tail[:, lanes], meta, blank], axis=0)
        tails = dot(collect, stacked).astype(BF)
        for a in range(NG):
            at = slice(a * 16, (a + 1) * 16)
            msg_ref[a * NY + y, 0:16, :] = key_main[at, lanes]
            msg_ref[a * NY + y, 16:32, :] = value_main[at, lanes]
            msg_ref[a * NY + y, 32:48, :] = tails[at]


def settle_qg_kernel(dest_ref, query_ref, grad_ref, msg_ref):
    main, tail = placing(dest_ref[...])
    main_b, tail_b = main.astype(BF), tail.astype(BF)
    perm = tail_perm(False)
    for y in range(NY):
        lanes = slice(y * GH * HD, (y + 1) * GH * HD)
        parts = []
        for index, ref in enumerate((query_ref, grad_ref)):
            block = ref[:, lanes]
            placed = dot(main_b, block).astype(BF)
            ends = dot(tail_b, block).astype(BF)
            for h in range(GH):
                s = index * GH + h
                parts.append(ends[:, h * HD : (h + 1) * HD])
                for a in range(NG):
                    msg_ref[a * NY + y, s * 16 : (s + 1) * 16, :] = placed[
                        a * 16 : (a + 1) * 16, h * HD : (h + 1) * HD
                    ]
        tails = dot(perm, jnp.concatenate(parts, axis=0)).astype(BF)
        for a in range(NG):
            msg_ref[a * NY + y, 256:288, :] = tails[a * 32 : (a + 1) * 32]


def arrange_kernel(msg_ref, chunk_ref):
    rows, cols = iota((48, 128), 0), iota((48, 128), 1)
    metas = jnp.zeros((16, 128), F32)
    for y in range(NY):
        base = y * PAIR
        for a in range(NG):
            chunk_ref[base + a * 16 : base + a * 16 + 16, :] = msg_ref[a * NY + y, 0:16, :]
            chunk_ref[base + SUB + a * 16 : base + SUB + a * 16 + 16, :] = msg_ref[
                a * NY + y, 16:32, :
            ]
        ends = jnp.concatenate([msg_ref[a * NY + y, 32:48, :] for a in range(NG)], axis=0)
        local = rows % 16
        want = (local // 2) * 16 + local % 2 + jnp.where(rows >= 16, 2, 0)
        want = jnp.where(rows < 32, want, -1)
        want = jnp.where((rows == 32 + y) & (cols % 16 == 4), cols, want)
        pick = cols == want
        got = dot(pick.astype(BF), ends)
        chunk_ref[base + 128 : base + 144, :] = got[0:16].astype(BF)
        chunk_ref[base + SUB + 128 : base + SUB + 144, :] = got[16:32].astype(BF)
        metas = metas + got[32:48]
    chunk_ref[2 * CHUNK :, :] = metas.astype(BF)


def sub_place(w):
    t = w - 128
    return jnp.where(w < 128, (w // 16) * CAP + w % 16, (t // 2) * CAP + MAIN + t % 2)


def label_of(place, meta, y):
    total = jnp.zeros(place.shape, F32)
    for c in range(3):
        total = total + (place >= meta[y : y + 1, c : c + 1]).astype(F32)
    return total


def attend_kernel(
    z_ref, qg_ref, c4_ref, c3_ref, c2_ref, c1_ref, c0_ref,
    msg_ref, r4_ref, r3_ref, r2_ref, r1_ref, r0_ref,
    kaug, value, qaug_t, grad_t, qplace, scores, weights, dkey, dvalue, outs, dqs,
):
    chunks = (c4_ref, c3_ref, c2_ref, c1_ref, c0_ref)
    lane = iota((1, 128), 1)
    lane_f = lane.astype(F32)
    place_w = sub_place(iota((SUB, 1), 0)).astype(F32)
    metas = [ref[2 * CHUNK :, :].astype(F32) for ref in chunks]

    for n, ref in enumerate(chunks):
        for y in range(NY):
            pair, at = 2 * n + y // 2, (y % 2) * SUB
            keys = ref[y * PAIR : y * PAIR + SUB, :]
            empty = (keys[:, 0:1].astype(F32) > 0.5 * EMPTY_KEY).astype(F32)
            label = label_of(place_w, metas[n], y)
            feature = jnp.where(
                lane < 4, (label == lane_f).astype(F32), jnp.where(lane == 4, empty, 0.0)
            )
            kaug[pair, at : at + SUB, 0:HD] = keys
            kaug[pair, at : at + SUB, HD:] = feature.astype(BF)
            value[pair, at : at + SUB, :] = ref[y * PAIR + SUB : (y + 1) * PAIR, :]
    dkey[...] = jnp.zeros(dkey.shape, F32)
    dvalue[...] = jnp.zeros(dvalue.shape, F32)

    perm = tail_perm(True)
    w256 = iota((TILE, 1), 0)
    main_place = (((w256 % 128) // 16) * CAP + w256 % 16).astype(F32)
    tail_place = (((w256 % 16) // 2) * CAP + MAIN + w256 % 2).astype(F32)
    j256 = iota((1, TILE), 1)
    main_lane = ((j256 % 128) // 16) * CAP + j256 % 16
    tail_lane = ((j256 % 16) // 2) * CAP + MAIN + j256 % 2 + jnp.where(j256 >= 128, SUB, 0)

    def features(label):
        wrong = jnp.where(label == lane_f, 0.0, -BIG)
        return jnp.where(lane < 4, wrong, jnp.where(lane == 4, -BIG, 0.0))

    def put(tile, query, grad, label, place):
        qaug_t[tile, 0:HD, :] = query.astype(F32).T.astype(BF)
        qaug_t[tile, HD:, :] = features(label).T.astype(BF)
        grad_t[tile, :, :] = grad.astype(F32).T.astype(BF)
        qplace[tile, :, :] = jnp.broadcast_to(place, (8, TILE))

    for u in range(2):
        tail_q, tail_g, tail_l = [], [], []
        for y in (2 * u, 2 * u + 1):
            label = label_of(main_place, metas[4], y)
            for hh in range(GH // 2):
                rows = [
                    jnp.concatenate(
                        [
                            qg_ref[a * NY + y, (s + h) * 16 : (s + h + 1) * 16, :]
                            for h in (2 * hh, 2 * hh + 1)
                            for a in range(NG)
                        ],
                        axis=0,
                    )
                    for s in (0, GH)
                ]
                put(9 * u + (y % 2) * 4 + hh, rows[0], rows[1], label, main_lane + (y % 2) * SUB)
            ends = jnp.concatenate([qg_ref[a * NY + y, 256:288, :] for a in range(NG)], axis=0)
            ends = dot(perm, ends).astype(BF)
            tail_q.append(ends[:128])
            tail_g.append(ends[128:])
            tail_l.append(label_of(tail_place[:128], metas[4], y))
        put(
            9 * u + 8,
            jnp.concatenate(tail_q, axis=0),
            jnp.concatenate(tail_g, axis=0),
            jnp.concatenate(tail_l, axis=0),
            tail_lane,
        )

    def count(mask):
        return jnp.sum(jnp.where((lane < 3) & mask, 1.0, 0.0)).astype(jnp.int32)

    lasts = [count(metas[p // 2][2 * (p % 2) + 1 : 2 * (p % 2) + 2, :] <= SUB - 1) for p in range(9)]
    reach = []
    for u in range(2):
        first = count(metas[4][2 * u : 2 * u + 1, :] <= 0)
        total = jnp.int32(0)
        for p in range(u, 8 + u):
            there = z_ref[0] * 2 + (p - 8) >= 0
            total = total + jnp.where(there & (lasts[p] == first), 1, 0)
        reach.append(total)

    key_place = iota((PAIR, 1), 0)
    key_place = sub_place(key_place % SUB) + (key_place // SUB) * SUB

    def tile_step(tile, carry):
        second = tile >= 9
        diag = jnp.where(second, 9, 8)
        begin = diag - jnp.where(second, reach[1], reach[0])

        def fold(x, op):
            return op(x.reshape(x.shape[0] // 8, 8, TILE), axis=0)

        s = dot(kaug[diag], qaug_t[tile])
        s = jnp.where(key_place <= qplace[tile][0:1, :], s, -4.0 * BIG)
        scores[diag] = s
        top = fold(s, jnp.max)

        def pass1(p, top):
            s = dot(kaug[p], qaug_t[tile])
            scores[p] = s
            return jnp.maximum(top, fold(s, jnp.max))

        top = lax.fori_loop(begin, diag, pass1, top)
        top = jnp.max(top, axis=0, keepdims=True)

        def pass2(p, carry):
            total, acc = carry
            for r in range(0, PAIR, SUB):
                e = jnp.exp2((scores[p, r : r + SUB, :] - top) * (SCALE * LOG2E))
                total = total + fold(e, jnp.sum)
                weights[p, r : r + SUB, :] = e.astype(BF)
            return total, acc + dot(value[p], weights[p], TN)

        zero = (jnp.zeros((8, TILE), F32), jnp.zeros((HD, TILE), F32))
        total, acc = lax.fori_loop(begin, diag + 1, pass2, zero)
        inverse = 1.0 / jnp.sum(total, axis=0, keepdims=True)
        out = (acc * inverse).astype(BF)
        outs[tile] = out.astype(F32).T.astype(BF)
        scaled = (grad_t[tile].astype(F32) * inverse).astype(BF)
        delta = jnp.sum(scaled.astype(F32) * out.astype(F32), axis=0, keepdims=True)

        def pass3(p, acc):
            dprod = dot(value[p], scaled)
            ds = (weights[p].astype(F32) * (dprod - delta)).astype(BF)
            dvalue[p] += dot(weights[p], scaled, NT)
            dkey[p] += dot(ds, qaug_t[tile, 0:HD, :], NT)
            return acc + dot(kaug[p, :, 0:HD], ds, TN)

        acc = lax.fori_loop(begin, diag + 1, pass3, jnp.zeros((HD, TILE), F32))
        dqs[tile] = (acc * SCALE).T.astype(BF)
        return carry

    lax.fori_loop(0, TILES, tile_step, 0)

    perm = tail_perm(False)
    for u in range(2):
        for y in (2 * u, 2 * u + 1):
            at = (y % 2) * 4
            for index, ref in enumerate((outs, dqs)):
                for h in range(GH):
                    s = index * GH + h
                    for a in range(NG):
                        row = (h % 2) * 128 + a * 16
                        msg_ref[a * NY + y, s * 16 : (s + 1) * 16, :] = ref[
                            9 * u + at + h // 2, row : row + 16, :
                        ]
            part = slice((y % 2) * 128, (y % 2 + 1) * 128)
            ends = jnp.concatenate([outs[9 * u + 8, part, :], dqs[9 * u + 8, part, :]], axis=0)
            ends = dot(perm, ends).astype(BF)
            for a in range(NG):
                msg_ref[a * NY + y, 256:288, :] = ends[a * 32 : (a + 1) * 32]
    for n, ref in enumerate((r4_ref, r3_ref, r2_ref, r1_ref, r0_ref)):
        for y in range(NY):
            pair, at = 2 * n + y // 2, (y % 2) * SUB
            ref[y * PAIR : y * PAIR + SUB, :] = (dkey[pair, at : at + SUB, :] * SCALE).astype(
                ref.dtype
            )
            ref[y * PAIR + SUB : (y + 1) * PAIR, :] = dvalue[pair, at : at + SUB, :].astype(
                ref.dtype
            )


def kv_back_kernel(own_ref, got_ref, msg_ref):
    for y in range(NY):
        base = y * PAIR
        both = own_ref[base : base + PAIR, :] + got_ref[base : base + PAIR, :].astype(F32)
        both = both.astype(BF)
        for a in range(NG):
            msg_ref[a * NY + y, 0:16, :] = both[a * 16 : a * 16 + 16]
            msg_ref[a * NY + y, 16:32, :] = both[SUB + a * 16 : SUB + a * 16 + 16]
            msg_ref[a * NY + y, 32:48, :] = both[128:144]
            msg_ref[a * NY + y, 48:64, :] = both[SUB + 128 : SUB + 144]


def unsettle_qg_kernel(dest_ref, msg_ref, out_ref, dq_ref):
    dest = dest_ref[...]
    rank = ranks(dest)
    at = jnp.where(rank < MAIN, dest * MAIN + rank, 128 + dest * 2 + rank - MAIN)
    pick = (iota((128, SUB), 1) == at).astype(BF)
    perm = tail_perm(True)
    for y in range(NY):
        ends = jnp.concatenate([msg_ref[g * NY + y, 256:288, :] for g in range(NG)], axis=0)
        ends = dot(perm, ends).astype(BF)
        for index, ref in enumerate((out_ref, dq_ref)):
            for h in range(GH):
                s = index * GH + h
                rows = [msg_ref[g * NY + y, s * 16 : (s + 1) * 16, :] for g in range(NG)]
                rows.append(ends[s * 16 : (s + 1) * 16])
                got = dot(pick, jnp.concatenate(rows, axis=0))
                col = (y * GH + h) * HD
                ref[:, col : col + HD] = got.astype(BF)


def unsettle_kv_kernel(grp_ref, dest_ref, msg_ref, dk_ref, dv_ref):
    dest = dest_ref[...]
    rank = ranks(dest)
    tail_at = 128 + dest * 16 + grp_ref[0] * 2 + rank - MAIN
    at = jnp.where(rank < MAIN, dest * MAIN + rank, tail_at)
    pick = (iota((128, 256), 1) == at).astype(BF)
    for y in range(NY):
        for index, ref in enumerate((dk_ref, dv_ref)):
            rows = [msg_ref[g * NY + y, 16 * index : 16 * index + 16, :] for g in range(NG)]
            rows += [msg_ref[g * NY + y, 32 + 16 * index : 48 + 16 * index, :] for g in range(NG)]
            got = dot(pick, jnp.concatenate(rows, axis=0))
            ref[:, y * HD : (y + 1) * HD] = got.astype(BF)


def call(kernel, outs, ins, scalars=0, scratch=(), flops=1000000, moved=1000000):
    smem = pl.BlockSpec(memory_space=pltpu.SMEM)
    vmem = pl.BlockSpec(memory_space=pltpu.VMEM)
    return pl.pallas_call(
        kernel,
        out_shape=[jax.ShapeDtypeStruct(s, d) for s, d in outs],
        in_specs=[smem] * scalars + [vmem] * (len(ins) - scalars),
        out_specs=[vmem] * len(outs),
        scratch_shapes=list(scratch),
        compiler_params=pltpu.CompilerParams(vmem_limit_bytes=VM),
        cost_estimate=pl.CostEstimate(flops=flops, bytes_accessed=moved, transcendentals=0),
    )(*ins)


def exchange(x):
    return lax.all_to_all(x, GY, split_axis=0, concat_axis=0, tiled=True)


def on_device(queries, key_rows, value_rows, out_grad, dest_group, slot_segment):
    grp = lax.axis_index("grp").astype(jnp.int32).reshape(1)
    z = lax.axis_index("z").astype(jnp.int32).reshape(1)
    onward = [(i, i + 1) for i in range(NZ - 1)]
    backward = [(i + 1, i) for i in range(NZ - 1)]
    (kv_msg,) = call(
        settle_kv_kernel,
        [((32, 48, HD), BF)],
        (grp, dest_group, key_rows, value_rows, slot_segment),
        scalars=1,
    )
    (qg_msg,) = call(settle_qg_kernel, [((32, PAIR, HD), BF)], (dest_group, queries, out_grad))
    kv_got = exchange(kv_msg)
    qg_got = exchange(qg_msg)
    (c0,) = call(arrange_kernel, [((2 * CHUNK + 16, HD), BF)], (kv_got,))
    c1 = lax.ppermute(c0, "z", onward)
    c2 = lax.ppermute(c1, "z", onward)
    c3 = lax.ppermute(c2, "z", onward)
    c4 = lax.ppermute(c3, "z", onward)
    part = ((2 * CHUNK, HD), BF)
    msg, r4, r3, r2, r1, r0 = call(
        attend_kernel,
        [((32, PAIR, HD), BF), part, part, part, part, ((2 * CHUNK, HD), F32)],
        (z, qg_got, c4, c3, c2, c1, c0),
        scalars=1,
        scratch=[
            pltpu.VMEM((PAIRS, PAIR, 2 * HD), BF),
            pltpu.VMEM((PAIRS, PAIR, HD), BF),
            pltpu.VMEM((TILES, 2 * HD, TILE), BF),
            pltpu.VMEM((TILES, HD, TILE), BF),
            pltpu.VMEM((TILES, 8, TILE), jnp.int32),
            pltpu.VMEM((PAIRS, PAIR, TILE), F32),
            pltpu.VMEM((PAIRS, PAIR, TILE), BF),
            pltpu.VMEM((PAIRS, PAIR, HD), F32),
            pltpu.VMEM((PAIRS, PAIR, HD), F32),
            pltpu.VMEM((TILES, TILE, HD), BF),
            pltpu.VMEM((TILES, TILE, HD), BF),
        ],
        flops=10**10,
        moved=10**7,
    )
    back = exchange(msg)
    moving = lax.ppermute(r4, "z", backward)
    for term in (r3, r2, r1):
        total = (moving.astype(F32) + term.astype(F32)).astype(BF)
        moving = lax.ppermute(total, "z", backward)
    (kv_back,) = call(kv_back_kernel, [((32, 64, HD), BF)], (r0, moving))
    kv_end = exchange(kv_back)
    rows = ((128, H * HD), BF)
    out, dq = call(unsettle_qg_kernel, [rows, rows], (dest_group, back))
    narrow = ((128, KV * HD), BF)
    dk, dv = call(unsettle_kv_kernel, [narrow, narrow], (grp, dest_group, kv_end), scalars=1)
    return out, dq, dk, dv


def solution(mesh):
    split = Mesh(mesh.devices.reshape(NG, NZ, NY), ("grp", "z", "y"))
    rows = P(("grp", "z", "y"), None)
    return jax.shard_map(
        on_device,
        mesh=split,
        in_specs=(rows, rows, rows, rows, rows, P("grp", ("z", "y"))),
        out_specs=(rows, rows, rows, rows),
        check_vma=False,
    )
```

```python
import math

import jax
import jax.numpy as jnp
from jax import lax
from jax.experimental import pallas as pl
from jax.experimental.pallas import tpu as pltpu
from jax.sharding import Mesh
from jax.sharding import PartitionSpec as P

H = 32
KV = 4
HD = 128
GH = H // KV
NG = 8
NZ = 8
NY = 4
CAP = 18
MAIN = 16
SUB = 144
PAIR = 288
CHUNK = 576
BACK = 4
PAIRS = 2 * (BACK + 1)
TILE = 256
TILES = 9
GT = 3
GROUPS = TILES // GT
WIDE = GT * TILE
BIG = 2.0**24
EMPTY_KEY = 64.0
SCALE = 1.0 / math.sqrt(HD)
LOG2E = 1.4426950408889634
GY = ("grp", "y")
BF = jnp.bfloat16
F32 = jnp.float32
NN = (((1,), (0,)), ((), ()))
NT = (((1,), (1,)), ((), ()))
TN = (((0,), (0,)), ((), ()))
VM = 56 * 1024 * 1024


def dot(a, b, dims=NN):
    return lax.dot_general(a, b, dims, preferred_element_type=F32)


def iota(shape, dim):
    return lax.broadcasted_iota(jnp.int32, shape, dim)


def ranks(dest):
    onehot = (dest == iota((128, 128), 1)).astype(F32)
    earlier = (iota((128, 128), 1) < iota((128, 128), 0)).astype(BF)
    counted = dot(earlier, onehot.astype(BF))
    return jnp.sum(counted * onehot, axis=1, keepdims=True).astype(jnp.int32)


def placing(dest):
    rank = ranks(dest)
    main_at = jnp.where(rank < MAIN, dest * MAIN + rank, -1)
    tail_at = jnp.where(rank >= MAIN, dest * 2 + rank - MAIN, -1)
    slots = iota((128, 128), 1)
    main = (slots == main_at).astype(F32).T
    tail = (slots == tail_at).astype(F32).T[:16]
    return main, tail


def tail_perm(by_slice):
    rows, cols = iota((256, 256), 0), iota((256, 256), 1)
    if by_slice:
        want = ((rows % 16) // 2) * 32 + (rows // 16) * 2 + rows % 2
    else:
        want = ((rows % 32) // 2) * 16 + (rows // 32) * 2 + rows % 2
    return (cols == want).astype(BF)


def settle_kv_kernel(grp_ref, dest_ref, key_ref, value_ref, seg_ref, msg_ref):
    main, tail = placing(dest_ref[...])
    main_b, tail_b = main.astype(BF), tail.astype(BF)
    empty_main = (1.0 - jnp.sum(main, axis=1, keepdims=True)) * EMPTY_KEY
    empty_tail = (1.0 - jnp.sum(tail, axis=1, keepdims=True)) * EMPTY_KEY
    key_main = (dot(main_b, key_ref[...]) + empty_main).astype(BF)
    key_tail = (dot(tail_b, key_ref[...]) + empty_tail).astype(BF)
    value_main = dot(main_b, value_ref[...]).astype(BF)
    value_tail = dot(tail_b, value_ref[...]).astype(BF)
    seg = seg_ref[...]
    lane = iota((1, 128), 1)
    meta = jnp.zeros((1, 128), F32)
    for c in range(3):
        below = jnp.sum((seg <= c).astype(F32), axis=1, keepdims=True)
        meta = jnp.where(lane == c, below, meta)
    meta = jnp.broadcast_to(meta, (16, 128)).astype(BF)
    rows, cols = iota((128, 128), 0), iota((128, 128), 1)
    owner, item = rows // 16, rows % 16
    want = jnp.where(item < 2, owner * 2 + item, 16 + owner * 2 + item - 2)
    want = jnp.where(item < 4, want, jnp.where((item == 4) & (owner == grp_ref[0]), 32, -1))
    collect = (cols == want).astype(BF)
    blank = jnp.zeros((80, 128), BF)
    for y in range(NY):
        lanes = slice(y * HD, (y + 1) * HD)
        stacked = jnp.concatenate([key_tail[:, lanes], value_tail[:, lanes], meta, blank], axis=0)
        tails = dot(collect, stacked).astype(BF)
        for a in range(NG):
            at = slice(a * 16, (a + 1) * 16)
            msg_ref[a * NY + y, 0:16, :] = key_main[at, lanes]
            msg_ref[a * NY + y, 16:32, :] = value_main[at, lanes]
            msg_ref[a * NY + y, 32:48, :] = tails[at]


def settle_qg_kernel(dest_ref, query_ref, grad_ref, msg_ref):
    main, tail = placing(dest_ref[...])
    main_b, tail_b = main.astype(BF), tail.astype(BF)
    perm = tail_perm(False)
    for y in range(NY):
        lanes = slice(y * GH * HD, (y + 1) * GH * HD)
        parts = []
        for index, ref in enumerate((query_ref, grad_ref)):
            block = ref[:, lanes]
            placed = dot(main_b, block).astype(BF)
            ends = dot(tail_b, block).astype(BF)
            for h in range(GH):
                s = index * GH + h
                parts.append(ends[:, h * HD : (h + 1) * HD])
                for a in range(NG):
                    msg_ref[a * NY + y, s * 16 : (s + 1) * 16, :] = placed[
                        a * 16 : (a + 1) * 16, h * HD : (h + 1) * HD
                    ]
        tails = dot(perm, jnp.concatenate(parts, axis=0)).astype(BF)
        for a in range(NG):
            msg_ref[a * NY + y, 256:288, :] = tails[a * 32 : (a + 1) * 32]


def arrange_kernel(msg_ref, pair0_ref, pair1_ref):
    rows, cols = iota((48, 128), 0), iota((48, 128), 1)
    for pair, ref in enumerate((pair0_ref, pair1_ref)):
        metas = jnp.zeros((16, 128), F32)
        for sub in range(2):
            y, base = 2 * pair + sub, sub * PAIR
            for a in range(NG):
                at = slice(base + a * 16, base + a * 16 + 16)
                ref[at, :] = msg_ref[a * NY + y, 0:16, :]
                at = slice(base + SUB + a * 16, base + SUB + a * 16 + 16)
                ref[at, :] = msg_ref[a * NY + y, 16:32, :]
            ends = jnp.concatenate([msg_ref[a * NY + y, 32:48, :] for a in range(NG)], axis=0)
            local = rows % 16
            want = (local // 2) * 16 + local % 2 + jnp.where(rows >= 16, 2, 0)
            want = jnp.where(rows < 32, want, -1)
            want = jnp.where((rows == 32 + sub) & (cols % 16 == 4), cols, want)
            got = dot((cols == want).astype(BF), ends)
            ref[base + 128 : base + 144, :] = got[0:16].astype(BF)
            ref[base + SUB + 128 : base + SUB + 144, :] = got[16:32].astype(BF)
            metas = metas + got[32:48]
        ref[2 * PAIR :, :] = metas.astype(BF)


def sub_place(w):
    t = w - 128
    return jnp.where(w < 128, (w // 16) * CAP + w % 16, (t // 2) * CAP + MAIN + t % 2)


def label_of(place, meta, sub):
    total = jnp.zeros(place.shape, F32)
    for c in range(3):
        total = total + (place >= meta[sub : sub + 1, c : c + 1]).astype(F32)
    return total


def attend_kernel(z_ref, qg_ref, *refs):
    pairs, msg_ref, backs = refs[:PAIRS], refs[PAIRS], refs[PAIRS + 1 : 2 * PAIRS + 1]
    kaug, value, qaug_t, grad_t, qplace, scores, weights, dkey, dvalue, outs, dqs = refs[
        2 * PAIRS + 1 :
    ]
    lane = iota((1, 128), 1)
    lane_f = lane.astype(F32)
    place_w = sub_place(iota((SUB, 1), 0)).astype(F32)
    metas = [ref[2 * PAIR :, :].astype(F32) for ref in pairs]

    for pair, ref in enumerate(pairs):
        for sub in range(2):
            at, base = sub * SUB, sub * PAIR
            keys = ref[base : base + SUB, :]
            empty = (keys[:, 0:1].astype(F32) > 0.5 * EMPTY_KEY).astype(F32)
            label = label_of(place_w, metas[pair], sub)
            feature = jnp.where(
                lane < 4, (label == lane_f).astype(F32), jnp.where(lane == 4, empty, 0.0)
            )
            kaug[pair, at : at + SUB, 0:HD] = keys
            kaug[pair, at : at + SUB, HD:] = feature.astype(BF)
            value[pair, at : at + SUB, :] = ref[base + SUB : base + PAIR, :]
    dkey[...] = jnp.zeros(dkey.shape, F32)
    dvalue[...] = jnp.zeros(dvalue.shape, F32)

    perm = tail_perm(True)
    j256 = iota((1, TILE), 1)
    main_lane = ((j256 % 128) // 16) * CAP + j256 % 16
    tail_lane = ((j256 % 16) // 2) * CAP + MAIN + j256 % 2

    feature_row = iota((HD, 1), 0)

    def put(u, tile, query, grad, label, place):
        g, at = u * GROUPS + tile // GT, slice((tile % GT) * TILE, (tile % GT + 1) * TILE)
        wrong = jnp.where(label == feature_row.astype(F32), 0.0, -BIG)
        feature = jnp.where(feature_row < 4, wrong, jnp.where(feature_row == 4, -BIG, 0.0))
        qaug_t[g, 0:HD, at] = query.T
        qaug_t[g, HD:, at] = feature.astype(BF)
        grad_t[g, :, at] = grad.T
        qplace[g, :, at] = jnp.broadcast_to(place, (8, TILE))

    for u in range(2):
        tail_q, tail_g, tail_l = [], [], []
        for y in (2 * u, 2 * u + 1):
            label = label_of(main_lane.astype(F32), metas[8 + u], y % 2)
            for hh in range(GH // 2):
                rows = [
                    jnp.concatenate(
                        [
                            qg_ref[a * NY + y, (s + h) * 16 : (s + h + 1) * 16, :]
                            for h in (2 * hh, 2 * hh + 1)
                            for a in range(NG)
                        ],
                        axis=0,
                    )
                    for s in (0, GH)
                ]
                put(u, (y % 2) * 4 + hh, rows[0], rows[1], label, main_lane + (y % 2) * SUB)
            ends = jnp.concatenate([qg_ref[a * NY + y, 256:288, :] for a in range(NG)], axis=0)
            ends = dot(perm, ends).astype(BF)
            tail_q.append(ends[:128])
            tail_g.append(ends[128:])
            tail_l.append(label_of(tail_lane.astype(F32), metas[8 + u], y % 2))
        put(
            u,
            8,
            jnp.concatenate(tail_q, axis=0),
            jnp.concatenate(tail_g, axis=0),
            jnp.where(j256 < 128, tail_l[0], tail_l[1]),
            tail_lane + jnp.where(j256 >= 128, SUB, 0),
        )

    def count(mask):
        return jnp.sum(jnp.where((lane < 3) & mask, 1.0, 0.0)).astype(jnp.int32)

    lasts = [count(metas[p][1:2, :] <= SUB - 1) for p in range(9)]
    reach = []
    for u in range(2):
        first = count(metas[8 + u][0:1, :] <= 0)
        total = jnp.int32(0)
        for p in range(u, 8 + u):
            there = z_ref[0] * 2 + (p - 8) >= 0
            total = total + jnp.where(there & (lasts[p] == first), 1, 0)
        reach.append(total)

    key_place = iota((PAIR, 1), 0)
    key_place = sub_place(key_place % SUB) + (key_place // SUB) * SUB

    def group_step(g, carry):
        second = g >= GROUPS
        diag = jnp.where(second, 9, 8)
        begin = diag - jnp.where(second, reach[1], reach[0])
        spans = [slice(t * TILE, (t + 1) * TILE) for t in range(GT)]

        def fold(x, op):
            return op(x.reshape(x.shape[0] // 8, 8, TILE), axis=0)

        tops = []
        for at in spans:
            s = dot(kaug[diag], qaug_t[g, :, at])
            s = jnp.where(key_place <= qplace[g, 0:1, at], s, -4.0 * BIG)
            scores[8, :, at] = s
            tops.append(fold(s, jnp.max))

        def span(ref, p, n, *rest):
            return ref[(pl.ds(p, n), *rest)].reshape(n * PAIR, -1)

        def sweep(body, begin, end, carry):
            for n in (4, 2, 1):
                steps = (end - begin) // n
                carry = lax.fori_loop(0, steps, lambda i, c, b=begin, n=n: body(b + n * i, n, c), carry)
                begin = begin + n * steps
            return carry

        def pass1(p, n, tops):
            new = []
            keys = span(kaug, p, n)
            for at, top in zip(spans, tops):
                s = dot(keys, qaug_t[g, :, at])
                scores[pl.ds(p - diag + 8, n), :, at] = s.reshape(n, PAIR, TILE)
                new.append(jnp.maximum(top, fold(s, jnp.max)))
            return tuple(new)

        tops = sweep(pass1, begin, diag, tuple(tops))
        tops = [jnp.max(top, axis=0, keepdims=True) for top in tops]

        def pass2(p, n, carry):
            new = []
            vals = span(value, p, n)
            for at, top, (total, acc) in zip(spans, tops, carry):
                parts = []
                for k in range(n):
                    for r in range(0, PAIR, SUB):
                        s = scores[p - diag + 8 + k, r : r + SUB, at]
                        e = jnp.exp2((s - top) * (SCALE * LOG2E))
                        total = total + fold(e, jnp.sum)
                        parts.append(e.astype(BF))
                e = jnp.concatenate(parts, axis=0)
                weights[pl.ds(p - diag + 8, n), :, at] = e.reshape(n, PAIR, TILE)
                new.append((total, acc + dot(vals, e, TN)))
            return tuple(new)

        zero = (jnp.zeros((8, TILE), F32), jnp.zeros((HD, TILE), F32))
        sums = sweep(pass2, begin, diag + 1, (zero,) * GT)
        scaled, deltas = [], []
        for at, (total, acc) in zip(spans, sums):
            inverse = 1.0 / jnp.sum(total, axis=0, keepdims=True)
            out = (acc * inverse).astype(BF)
            outs[g, at, :] = out.T
            grad = (grad_t[g, :, at].astype(F32) * inverse).astype(BF)
            deltas.append(jnp.sum(grad.astype(F32) * out.astype(F32), axis=0, keepdims=True))
            scaled.append(grad)

        def pass3(p, n, accs):
            new, dk, dv = [], 0.0, 0.0
            vals = span(value, p, n)
            keys = span(kaug, p, n, slice(None), slice(0, HD))
            for at, grad, delta, acc in zip(spans, scaled, deltas, accs):
                dprod = dot(vals, grad)
                w = span(weights, p - diag + 8, n, slice(None), at)
                ds = (w.astype(F32) * (dprod - delta)).astype(BF)
                dv = dv + dot(w, grad, NT)
                dk = dk + dot(ds, qaug_t[g, 0:HD, at], NT)
                new.append(acc + dot(keys, ds, TN))
            dvalue[pl.ds(p, n)] += dv.reshape(n, PAIR, HD)
            dkey[pl.ds(p, n)] += dk.reshape(n, PAIR, HD)
            return tuple(new)

        accs = sweep(pass3, begin, diag + 1, (jnp.zeros((HD, TILE), F32),) * GT)
        for at, acc in zip(spans, accs):
            dqs[g, at, :] = (acc * SCALE).astype(BF).T
        return carry

    lax.fori_loop(0, 2 * GROUPS, group_step, 0)

    perm = tail_perm(False)
    for u in range(2):
        for y in (2 * u, 2 * u + 1):
            at = (y % 2) * 4
            for index, ref in enumerate((outs, dqs)):
                for h in range(GH):
                    s = index * GH + h
                    for a in range(NG):
                        tile = at + h // 2
                        row = (tile % GT) * TILE + (h % 2) * 128 + a * 16
                        msg_ref[a * NY + y, s * 16 : (s + 1) * 16, :] = ref[
                            u * GROUPS + tile // GT, row : row + 16, :
                        ]
            last = (GT - 1) * TILE + (y % 2) * 128
            ends = [ref[u * GROUPS + GROUPS - 1, last : last + 128, :] for ref in (outs, dqs)]
            ends = jnp.concatenate(ends, axis=0)
            ends = dot(perm, ends).astype(BF)
            for a in range(NG):
                msg_ref[a * NY + y, 256:288, :] = ends[a * 32 : (a + 1) * 32]
    for pair, ref in enumerate(backs):
        for sub in range(2):
            at, base = sub * SUB, sub * PAIR
            keys = dkey[pair, at : at + SUB, :] * SCALE
            ref[base : base + SUB, :] = keys.astype(ref.dtype)
            ref[base + SUB : base + PAIR, :] = dvalue[pair, at : at + SUB, :].astype(ref.dtype)


def kv_back_kernel(own0_ref, own1_ref, got0_ref, got1_ref, msg_ref):
    for pair, (own, got) in enumerate(((own0_ref, got0_ref), (own1_ref, got1_ref))):
        for sub in range(2):
            y, base = 2 * pair + sub, sub * PAIR
            both = own[base : base + PAIR, :] + got[base : base + PAIR, :].astype(F32)
            both = both.astype(BF)
            for a in range(NG):
                msg_ref[a * NY + y, 0:16, :] = both[a * 16 : a * 16 + 16]
                msg_ref[a * NY + y, 16:32, :] = both[SUB + a * 16 : SUB + a * 16 + 16]
                msg_ref[a * NY + y, 32:48, :] = both[128:144]
                msg_ref[a * NY + y, 48:64, :] = both[SUB + 128 : SUB + 144]


def unsettle_qg_kernel(dest_ref, msg_ref, out_ref, dq_ref):
    dest = dest_ref[...]
    rank = ranks(dest)
    at = jnp.where(rank < MAIN, dest * MAIN + rank, 128 + dest * 2 + rank - MAIN)
    pick = (iota((128, SUB), 1) == at).astype(BF)
    perm = tail_perm(True)
    for y in range(NY):
        ends = jnp.concatenate([msg_ref[g * NY + y, 256:288, :] for g in range(NG)], axis=0)
        ends = dot(perm, ends).astype(BF)
        for index, ref in enumerate((out_ref, dq_ref)):
            for h in range(GH):
                s = index * GH + h
                rows = [msg_ref[g * NY + y, s * 16 : (s + 1) * 16, :] for g in range(NG)]
                rows.append(ends[s * 16 : (s + 1) * 16])
                got = dot(pick, jnp.concatenate(rows, axis=0))
                col = (y * GH + h) * HD
                ref[:, col : col + HD] = got.astype(BF)


def unsettle_kv_kernel(grp_ref, dest_ref, msg_ref, dk_ref, dv_ref):
    dest = dest_ref[...]
    rank = ranks(dest)
    tail_at = 128 + dest * 16 + grp_ref[0] * 2 + rank - MAIN
    at = jnp.where(rank < MAIN, dest * MAIN + rank, tail_at)
    pick = (iota((128, 256), 1) == at).astype(BF)
    for y in range(NY):
        for index, ref in enumerate((dk_ref, dv_ref)):
            rows = [msg_ref[g * NY + y, 16 * index : 16 * index + 16, :] for g in range(NG)]
            rows += [msg_ref[g * NY + y, 32 + 16 * index : 48 + 16 * index, :] for g in range(NG)]
            got = dot(pick, jnp.concatenate(rows, axis=0))
            ref[:, y * HD : (y + 1) * HD] = got.astype(BF)


def call(kernel, outs, ins, scalars=0, scratch=(), flops=1000000, moved=1000000):
    smem = pl.BlockSpec(memory_space=pltpu.SMEM)
    vmem = pl.BlockSpec(memory_space=pltpu.VMEM)
    return pl.pallas_call(
        kernel,
        out_shape=[jax.ShapeDtypeStruct(s, d) for s, d in outs],
        in_specs=[smem] * scalars + [vmem] * (len(ins) - scalars),
        out_specs=[vmem] * len(outs),
        scratch_shapes=list(scratch),
        compiler_params=pltpu.CompilerParams(vmem_limit_bytes=VM),
        cost_estimate=pl.CostEstimate(flops=flops, bytes_accessed=moved, transcendentals=0),
    )(*ins)


def exchange(x):
    return lax.all_to_all(x, GY, split_axis=0, concat_axis=0, tiled=True)


def attend(z, qg_got, *pairs):
    part = (2 * PAIR, HD)
    parts = [(part, BF)] * (PAIRS - 2) + [(part, F32)] * 2
    return call(
        attend_kernel,
        [((32, PAIR, HD), BF)] + parts,
        (z, qg_got, *pairs),
        scalars=1,
        scratch=[
            pltpu.VMEM((PAIRS, PAIR, 2 * HD), BF),
            pltpu.VMEM((PAIRS, PAIR, HD), BF),
            pltpu.VMEM((2 * GROUPS, 2 * HD, WIDE), BF),
            pltpu.VMEM((2 * GROUPS, HD, WIDE), BF),
            pltpu.VMEM((2 * GROUPS, 8, WIDE), jnp.int32),
            pltpu.VMEM((PAIRS - 1, PAIR, WIDE), F32),
            pltpu.VMEM((PAIRS - 1, PAIR, WIDE), BF),
            pltpu.VMEM((PAIRS, PAIR, HD), F32),
            pltpu.VMEM((PAIRS, PAIR, HD), F32),
            pltpu.VMEM((2 * GROUPS, WIDE, HD), BF),
            pltpu.VMEM((2 * GROUPS, WIDE, HD), BF),
        ],
        flops=10**10,
        moved=10**7,
    )


def on_device(queries, key_rows, value_rows, out_grad, dest_group, slot_segment):
    grp = lax.axis_index("grp").astype(jnp.int32).reshape(1)
    z = lax.axis_index("z").astype(jnp.int32).reshape(1)
    onward = [(i, i + 1) for i in range(NZ - 1)]
    backward = [(i + 1, i) for i in range(NZ - 1)]
    (kv_msg,) = call(
        settle_kv_kernel,
        [((32, 48, HD), BF)],
        (grp, dest_group, key_rows, value_rows, slot_segment),
        scalars=1,
    )
    (qg_msg,) = call(settle_qg_kernel, [((32, PAIR, HD), BF)], (dest_group, queries, out_grad))
    kv_got = exchange(kv_msg)
    own = call(arrange_kernel, [((2 * PAIR + 16, HD), BF)] * 2, (kv_got,))
    *own, qg_msg = lax.optimization_barrier((*own, qg_msg))
    qg_got = exchange(qg_msg)
    pairs = list(own)
    for _ in range(BACK):
        pairs = [lax.ppermute(x, "z", onward) for x in pairs[:2]] + pairs
    msg, *backs = attend(z, qg_got, *pairs)
    back = exchange(msg)
    moving = [lax.ppermute(x, "z", backward) for x in backs[:2]]
    for n in range(1, BACK):
        terms = backs[2 * n : 2 * n + 2]
        total = [(m.astype(F32) + t.astype(F32)).astype(BF) for m, t in zip(moving, terms)]
        moving = [lax.ppermute(x, "z", backward) for x in total]
    *moving, back = lax.optimization_barrier((*moving, back))
    (kv_back,) = call(kv_back_kernel, [((32, 64, HD), BF)], (*backs[-2:], *moving))
    kv_end = exchange(kv_back)
    rows = ((128, H * HD), BF)
    out, dq = call(unsettle_qg_kernel, [rows, rows], (dest_group, back))
    narrow = ((128, KV * HD), BF)
    dk, dv = call(unsettle_kv_kernel, [narrow, narrow], (grp, dest_group, kv_end), scalars=1)
    return out, dq, dk, dv


def solution(mesh):
    split = Mesh(mesh.devices.reshape(NG, NZ, NY), ("grp", "z", "y"))
    rows = P(("grp", "z", "y"), None)
    return jax.shard_map(
        on_device,
        mesh=split,
        in_specs=(rows, rows, rows, rows, rows, P("grp", ("z", "y"))),
        out_specs=(rows, rows, rows, rows),
        check_vma=False,
    )
```

```python
import math

import jax
import jax.numpy as jnp
from jax import lax
from jax.experimental import pallas as pl
from jax.experimental.pallas import tpu as pltpu
from jax.sharding import Mesh
from jax.sharding import PartitionSpec as P

H = 32
KV = 4
HD = 128
GH = H // KV
NG = 8
NZ = 8
NY = 4
CAP = 18
MAIN = 16
SUB = 144
PAIR = 288
CHUNK = 576
BACK = 4
PAIRS = 2 * (BACK + 1)
TILE = 256
TILES = 9
GT = 3
GROUPS = TILES // GT
WIDE = GT * TILE
BIG = 2.0**24
EMPTY_KEY = 64.0
SCALE = 1.0 / math.sqrt(HD)
LOG2E = 1.4426950408889634
GY = ("grp", "y")
BF = jnp.bfloat16
F32 = jnp.float32
NN = (((1,), (0,)), ((), ()))
NT = (((1,), (1,)), ((), ()))
TN = (((0,), (0,)), ((), ()))
VM = 56 * 1024 * 1024
VM_FEW = 16 * 1024 * 1024


def dot(a, b, dims=NN):
    return lax.dot_general(a, b, dims, preferred_element_type=F32)


def iota(shape, dim):
    return lax.broadcasted_iota(jnp.int32, shape, dim)


def column(dest_ref):
    wide = jnp.broadcast_to(dest_ref[...].astype(F32), (128, 128))
    return wide.T[:, 0:1].astype(jnp.int32)


def ranks(dest):
    onehot = (dest == iota((128, 128), 1)).astype(F32)
    earlier = (iota((128, 128), 1) < iota((128, 128), 0)).astype(BF)
    counted = dot(earlier, onehot.astype(BF))
    return jnp.sum(counted * onehot, axis=1, keepdims=True).astype(jnp.int32)


def placing(dest):
    rank = ranks(dest)
    main_at = jnp.where(rank < MAIN, dest * MAIN + rank, -1)
    tail_at = jnp.where(rank >= MAIN, dest * 2 + rank - MAIN, -1)
    slots = iota((128, 128), 1)
    main = (slots == main_at).astype(F32).T
    tail = (slots == tail_at).astype(F32).T[:16]
    return main, tail


def tail_perm(by_slice):
    rows, cols = iota((256, 256), 0), iota((256, 256), 1)
    if by_slice:
        want = ((rows % 16) // 2) * 32 + (rows // 16) * 2 + rows % 2
    else:
        want = ((rows % 32) // 2) * 16 + (rows // 32) * 2 + rows % 2
    return (cols == want).astype(BF)


def settle_kv_kernel(grp_ref, dest_ref, key_ref, value_ref, seg_ref, msg_ref):
    main, tail = placing(column(dest_ref))
    main_b, tail_b = main.astype(BF), tail.astype(BF)
    empty_main = (1.0 - jnp.sum(main, axis=1, keepdims=True)) * EMPTY_KEY
    empty_tail = (1.0 - jnp.sum(tail, axis=1, keepdims=True)) * EMPTY_KEY
    key_main = (dot(main_b, key_ref[...]) + empty_main).astype(BF)
    key_tail = (dot(tail_b, key_ref[...]) + empty_tail).astype(BF)
    value_main = dot(main_b, value_ref[...]).astype(BF)
    value_tail = dot(tail_b, value_ref[...]).astype(BF)
    seg = seg_ref[...]
    lane = iota((1, 128), 1)
    meta = jnp.zeros((1, 128), F32)
    for c in range(3):
        below = jnp.sum((seg <= c).astype(F32), axis=1, keepdims=True)
        meta = jnp.where(lane == c, below, meta)
    meta = jnp.broadcast_to(meta, (16, 128)).astype(BF)
    rows, cols = iota((128, 128), 0), iota((128, 128), 1)
    owner, item = rows // 16, rows % 16
    want = jnp.where(item < 2, owner * 2 + item, 16 + owner * 2 + item - 2)
    want = jnp.where(item < 4, want, jnp.where((item == 4) & (owner == grp_ref[0]), 32, -1))
    collect = (cols == want).astype(BF)
    blank = jnp.zeros((80, 128), BF)
    for y in range(NY):
        lanes = slice(y * HD, (y + 1) * HD)
        stacked = jnp.concatenate([key_tail[:, lanes], value_tail[:, lanes], meta, blank], axis=0)
        tails = dot(collect, stacked).astype(BF)
        for a in range(NG):
            at = slice(a * 16, (a + 1) * 16)
            msg_ref[a * NY + y, 0:16, :] = key_main[at, lanes]
            msg_ref[a * NY + y, 16:32, :] = value_main[at, lanes]
            msg_ref[a * NY + y, 32:48, :] = tails[at]


def settle_qg_kernel(dest_ref, query_ref, grad_ref, msg_ref):
    main, tail = placing(column(dest_ref))
    main_b, tail_b = main.astype(BF), tail.astype(BF)
    perm = tail_perm(False)
    for y in range(NY):
        lanes = slice(y * GH * HD, (y + 1) * GH * HD)
        parts = []
        for index, ref in enumerate((query_ref, grad_ref)):
            block = ref[:, lanes]
            placed = dot(main_b, block).astype(BF)
            ends = dot(tail_b, block).astype(BF)
            for h in range(GH):
                s = index * GH + h
                parts.append(ends[:, h * HD : (h + 1) * HD])
                for a in range(NG):
                    msg_ref[a * NY + y, s * 16 : (s + 1) * 16, :] = placed[
                        a * 16 : (a + 1) * 16, h * HD : (h + 1) * HD
                    ]
        tails = dot(perm, jnp.concatenate(parts, axis=0)).astype(BF)
        for a in range(NG):
            msg_ref[a * NY + y, 256:288, :] = tails[a * 32 : (a + 1) * 32]


def arrange_kernel(msg_ref, pair0_ref, pair1_ref):
    rows, cols = iota((48, 128), 0), iota((48, 128), 1)
    for pair, ref in enumerate((pair0_ref, pair1_ref)):
        metas = jnp.zeros((16, 128), F32)
        for sub in range(2):
            y, base = 2 * pair + sub, sub * PAIR
            for a in range(NG):
                at = slice(base + a * 16, base + a * 16 + 16)
                ref[at, :] = msg_ref[a * NY + y, 0:16, :]
                at = slice(base + SUB + a * 16, base + SUB + a * 16 + 16)
                ref[at, :] = msg_ref[a * NY + y, 16:32, :]
            ends = jnp.concatenate([msg_ref[a * NY + y, 32:48, :] for a in range(NG)], axis=0)
            local = rows % 16
            want = (local // 2) * 16 + local % 2 + jnp.where(rows >= 16, 2, 0)
            want = jnp.where(rows < 32, want, -1)
            want = jnp.where((rows == 32 + sub) & (cols % 16 == 4), cols, want)
            got = dot((cols == want).astype(BF), ends)
            ref[base + 128 : base + 144, :] = got[0:16].astype(BF)
            ref[base + SUB + 128 : base + SUB + 144, :] = got[16:32].astype(BF)
            metas = metas + got[32:48]
        ref[2 * PAIR :, :] = metas.astype(BF)


def sub_place(w):
    t = w - 128
    return jnp.where(w < 128, (w // 16) * CAP + w % 16, (t // 2) * CAP + MAIN + t % 2)


def label_of(place, meta, sub):
    total = jnp.zeros(place.shape, F32)
    for c in range(3):
        total = total + (place >= meta[sub : sub + 1, c : c + 1]).astype(F32)
    return total


def attend_kernel(z_ref, qg_ref, *refs):
    pairs, msg_ref, backs = refs[:PAIRS], refs[PAIRS], refs[PAIRS + 1 : 2 * PAIRS + 1]
    kaug, value, qaug_t, grad_t, qplace, scores, weights, dkey, dvalue, outs, dqs = refs[
        2 * PAIRS + 1 :
    ]
    lane = iota((1, 128), 1)
    lane_f = lane.astype(F32)
    place_w = sub_place(iota((SUB, 1), 0)).astype(F32)
    metas = [ref[2 * PAIR :, :].astype(F32) for ref in pairs]

    for pair, ref in enumerate(pairs):
        for sub in range(2):
            at, base = sub * SUB, sub * PAIR
            keys = ref[base : base + SUB, :]
            empty = (keys[:, 0:1].astype(F32) > 0.5 * EMPTY_KEY).astype(F32)
            label = label_of(place_w, metas[pair], sub)
            feature = jnp.where(
                lane < 4, (label == lane_f).astype(F32), jnp.where(lane == 4, empty, 0.0)
            )
            kaug[pair, at : at + SUB, 0:HD] = keys
            kaug[pair, at : at + SUB, HD:] = feature.astype(BF)
            value[pair, at : at + SUB, :] = ref[base + SUB : base + PAIR, :]
    dkey[...] = jnp.zeros(dkey.shape, F32)
    dvalue[...] = jnp.zeros(dvalue.shape, F32)

    perm = tail_perm(True)
    j256 = iota((1, TILE), 1)
    main_lane = ((j256 % 128) // 16) * CAP + j256 % 16
    tail_lane = ((j256 % 16) // 2) * CAP + MAIN + j256 % 2

    feature_row = iota((HD, 1), 0)

    def put(u, tile, query, grad, label, place):
        g, at = u * GROUPS + tile // GT, slice((tile % GT) * TILE, (tile % GT + 1) * TILE)
        wrong = jnp.where(label == feature_row.astype(F32), 0.0, -BIG)
        feature = jnp.where(feature_row < 4, wrong, jnp.where(feature_row == 4, -BIG, 0.0))
        qaug_t[g, 0:HD, at] = query.T
        qaug_t[g, HD:, at] = feature.astype(BF)
        grad_t[g, :, at] = grad.T
        qplace[g, :, at] = jnp.broadcast_to(place, (8, TILE))

    for u in range(2):
        tail_q, tail_g, tail_l = [], [], []
        for y in (2 * u, 2 * u + 1):
            label = label_of(main_lane.astype(F32), metas[8 + u], y % 2)
            for hh in range(GH // 2):
                rows = [
                    jnp.concatenate(
                        [
                            qg_ref[a * NY + y, (s + h) * 16 : (s + h + 1) * 16, :]
                            for h in (2 * hh, 2 * hh + 1)
                            for a in range(NG)
                        ],
                        axis=0,
                    )
                    for s in (0, GH)
                ]
                put(u, (y % 2) * 4 + hh, rows[0], rows[1], label, main_lane + (y % 2) * SUB)
            ends = jnp.concatenate([qg_ref[a * NY + y, 256:288, :] for a in range(NG)], axis=0)
            ends = dot(perm, ends).astype(BF)
            tail_q.append(ends[:128])
            tail_g.append(ends[128:])
            tail_l.append(label_of(tail_lane.astype(F32), metas[8 + u], y % 2))
        put(
            u,
            8,
            jnp.concatenate(tail_q, axis=0),
            jnp.concatenate(tail_g, axis=0),
            jnp.where(j256 < 128, tail_l[0], tail_l[1]),
            tail_lane + jnp.where(j256 >= 128, SUB, 0),
        )

    def count(mask):
        return jnp.sum(jnp.where((lane < 3) & mask, 1.0, 0.0)).astype(jnp.int32)

    lasts = [count(metas[p][1:2, :] <= SUB - 1) for p in range(9)]
    reach = []
    for u in range(2):
        first = count(metas[8 + u][0:1, :] <= 0)
        total = jnp.int32(0)
        for p in range(u, 8 + u):
            there = z_ref[0] * 2 + (p - 8) >= 0
            total = total + jnp.where(there & (lasts[p] == first), 1, 0)
        reach.append(total)

    key_place = iota((PAIR, 1), 0)
    key_place = sub_place(key_place % SUB) + (key_place // SUB) * SUB

    def group_step(g, carry):
        second = g >= GROUPS
        diag = jnp.where(second, 9, 8)
        begin = diag - jnp.where(second, reach[1], reach[0])
        spans = [slice(t * TILE, (t + 1) * TILE) for t in range(GT)]

        def fold(x, op):
            return op(x.reshape(x.shape[0] // 8, 8, TILE), axis=0)

        tops = []
        for at in spans:
            s = dot(kaug[diag], qaug_t[g, :, at])
            s = jnp.where(key_place <= qplace[g, 0:1, at], s, -4.0 * BIG)
            scores[8, :, at] = s
            tops.append(fold(s, jnp.max))

        def span(ref, p, n, *rest):
            return ref[(pl.ds(p, n), *rest)].reshape(n * PAIR, -1)

        def sweep(body, begin, end, carry):
            for n in (4, 2, 1):
                steps = (end - begin) // n
                carry = lax.fori_loop(0, steps, lambda i, c, b=begin, n=n: body(b + n * i, n, c), carry)
                begin = begin + n * steps
            return carry

        def pass1(p, n, tops):
            new = []
            keys = span(kaug, p, n)
            for at, top in zip(spans, tops):
                s = dot(keys, qaug_t[g, :, at])
                scores[pl.ds(p - diag + 8, n), :, at] = s.reshape(n, PAIR, TILE)
                new.append(jnp.maximum(top, fold(s, jnp.max)))
            return tuple(new)

        tops = sweep(pass1, begin, diag, tuple(tops))
        tops = [jnp.max(top, axis=0, keepdims=True) for top in tops]

        def pass2(p, n, carry):
            new = []
            vals = span(value, p, n)
            for at, top, (total, acc) in zip(spans, tops, carry):
                parts = []
                for k in range(n):
                    for r in range(0, PAIR, SUB):
                        s = scores[p - diag + 8 + k, r : r + SUB, at]
                        e = jnp.exp2((s - top) * (SCALE * LOG2E))
                        total = total + fold(e, jnp.sum)
                        parts.append(e.astype(BF))
                e = jnp.concatenate(parts, axis=0)
                weights[pl.ds(p - diag + 8, n), :, at] = e.reshape(n, PAIR, TILE)
                new.append((total, acc + dot(vals, e, TN)))
            return tuple(new)

        zero = (jnp.zeros((8, TILE), F32), jnp.zeros((HD, TILE), F32))
        sums = sweep(pass2, begin, diag + 1, (zero,) * GT)
        scaled, deltas = [], []
        for at, (total, acc) in zip(spans, sums):
            inverse = 1.0 / jnp.sum(total, axis=0, keepdims=True)
            out = (acc * inverse).astype(BF)
            outs[g, at, :] = out.T
            grad = (grad_t[g, :, at].astype(F32) * inverse).astype(BF)
            deltas.append(jnp.sum(grad.astype(F32) * out.astype(F32), axis=0, keepdims=True))
            scaled.append(grad)

        def pass3(p, n, accs):
            new, dk, dv = [], 0.0, 0.0
            vals = span(value, p, n)
            keys = span(kaug, p, n, slice(None), slice(0, HD))
            for at, grad, delta, acc in zip(spans, scaled, deltas, accs):
                dprod = dot(vals, grad)
                w = span(weights, p - diag + 8, n, slice(None), at)
                ds = (w.astype(F32) * (dprod - delta)).astype(BF)
                dv = dv + dot(w, grad, NT)
                dk = dk + dot(ds, qaug_t[g, 0:HD, at], NT)
                new.append(acc + dot(keys, ds, TN))
            dvalue[pl.ds(p, n)] += dv.reshape(n, PAIR, HD)
            dkey[pl.ds(p, n)] += dk.reshape(n, PAIR, HD)
            return tuple(new)

        accs = sweep(pass3, begin, diag + 1, (jnp.zeros((HD, TILE), F32),) * GT)
        for at, acc in zip(spans, accs):
            dqs[g, at, :] = (acc * SCALE).astype(BF).T
        return carry

    lax.fori_loop(0, 2 * GROUPS, group_step, 0)

    perm = tail_perm(False)
    for u in range(2):
        for y in (2 * u, 2 * u + 1):
            at = (y % 2) * 4
            for index, ref in enumerate((outs, dqs)):
                for h in range(GH):
                    s = index * GH + h
                    for a in range(NG):
                        tile = at + h // 2
                        row = (tile % GT) * TILE + (h % 2) * 128 + a * 16
                        msg_ref[a * NY + y, s * 16 : (s + 1) * 16, :] = ref[
                            u * GROUPS + tile // GT, row : row + 16, :
                        ]
            last = (GT - 1) * TILE + (y % 2) * 128
            ends = [ref[u * GROUPS + GROUPS - 1, last : last + 128, :] for ref in (outs, dqs)]
            ends = jnp.concatenate(ends, axis=0)
            ends = dot(perm, ends).astype(BF)
            for a in range(NG):
                msg_ref[a * NY + y, 256:288, :] = ends[a * 32 : (a + 1) * 32]
    for pair, ref in enumerate(backs):
        for sub in range(2):
            at, base = sub * SUB, sub * PAIR
            keys = dkey[pair, at : at + SUB, :] * SCALE
            ref[base : base + SUB, :] = keys.astype(ref.dtype)
            ref[base + SUB : base + PAIR, :] = dvalue[pair, at : at + SUB, :].astype(ref.dtype)


def kv_back_kernel(own0_ref, own1_ref, got0_ref, got1_ref, msg_ref):
    for pair, (own, got) in enumerate(((own0_ref, got0_ref), (own1_ref, got1_ref))):
        for sub in range(2):
            y, base = 2 * pair + sub, sub * PAIR
            both = own[base : base + PAIR, :] + got[base : base + PAIR, :].astype(F32)
            both = both.astype(BF)
            for a in range(NG):
                msg_ref[a * NY + y, 0:16, :] = both[a * 16 : a * 16 + 16]
                msg_ref[a * NY + y, 16:32, :] = both[SUB + a * 16 : SUB + a * 16 + 16]
                msg_ref[a * NY + y, 32:48, :] = both[128:144]
                msg_ref[a * NY + y, 48:64, :] = both[SUB + 128 : SUB + 144]


def unsettle_qg_kernel(dest_ref, msg_ref, out_ref, dq_ref):
    dest = column(dest_ref)
    rank = ranks(dest)
    at = jnp.where(rank < MAIN, dest * MAIN + rank, 128 + dest * 2 + rank - MAIN)
    pick = (iota((128, SUB), 1) == at).astype(BF)
    perm = tail_perm(True)
    for y in range(NY):
        ends = jnp.concatenate([msg_ref[g * NY + y, 256:288, :] for g in range(NG)], axis=0)
        ends = dot(perm, ends).astype(BF)
        for index, ref in enumerate((out_ref, dq_ref)):
            for h in range(GH):
                s = index * GH + h
                rows = [msg_ref[g * NY + y, s * 16 : (s + 1) * 16, :] for g in range(NG)]
                rows.append(ends[s * 16 : (s + 1) * 16])
                got = dot(pick, jnp.concatenate(rows, axis=0))
                col = (y * GH + h) * HD
                ref[:, col : col + HD] = got.astype(BF)


def unsettle_kv_kernel(grp_ref, dest_ref, msg_ref, dk_ref, dv_ref):
    dest = column(dest_ref)
    rank = ranks(dest)
    tail_at = 128 + dest * 16 + grp_ref[0] * 2 + rank - MAIN
    at = jnp.where(rank < MAIN, dest * MAIN + rank, tail_at)
    pick = (iota((128, 256), 1) == at).astype(BF)
    for y in range(NY):
        for index, ref in enumerate((dk_ref, dv_ref)):
            rows = [msg_ref[g * NY + y, 16 * index : 16 * index + 16, :] for g in range(NG)]
            rows += [msg_ref[g * NY + y, 32 + 16 * index : 48 + 16 * index, :] for g in range(NG)]
            got = dot(pick, jnp.concatenate(rows, axis=0))
            ref[:, y * HD : (y + 1) * HD] = got.astype(BF)


def call(kernel, outs, ins, scalars=0, scratch=(), vm=VM, flops=1000000, moved=1000000):
    smem = pl.BlockSpec(memory_space=pltpu.SMEM)
    vmem = pl.BlockSpec(memory_space=pltpu.VMEM)
    return pl.pallas_call(
        kernel,
        out_shape=[jax.ShapeDtypeStruct(s, d) for s, d in outs],
        in_specs=[smem] * scalars + [vmem] * (len(ins) - scalars),
        out_specs=[vmem] * len(outs),
        scratch_shapes=list(scratch),
        compiler_params=pltpu.CompilerParams(vmem_limit_bytes=vm),
        cost_estimate=pl.CostEstimate(flops=flops, bytes_accessed=moved, transcendentals=0),
    )(*ins)


def exchange(x):
    return lax.all_to_all(x, GY, split_axis=0, concat_axis=0, tiled=True)


def attend(z, qg_got, *pairs):
    part = (2 * PAIR, HD)
    parts = [(part, BF)] * (PAIRS - 2) + [(part, F32)] * 2
    return call(
        attend_kernel,
        [((32, PAIR, HD), BF)] + parts,
        (z, qg_got, *pairs),
        scalars=1,
        scratch=[
            pltpu.VMEM((PAIRS, PAIR, 2 * HD), BF),
            pltpu.VMEM((PAIRS, PAIR, HD), BF),
            pltpu.VMEM((2 * GROUPS, 2 * HD, WIDE), BF),
            pltpu.VMEM((2 * GROUPS, HD, WIDE), BF),
            pltpu.VMEM((2 * GROUPS, 8, WIDE), jnp.int32),
            pltpu.VMEM((PAIRS - 1, PAIR, WIDE), F32),
            pltpu.VMEM((PAIRS - 1, PAIR, WIDE), BF),
            pltpu.VMEM((PAIRS, PAIR, HD), F32),
            pltpu.VMEM((PAIRS, PAIR, HD), F32),
            pltpu.VMEM((2 * GROUPS, WIDE, HD), BF),
            pltpu.VMEM((2 * GROUPS, WIDE, HD), BF),
        ],
        flops=10**10,
        moved=10**7,
    )


def on_device(queries, key_rows, value_rows, out_grad, dest_group, slot_segment):
    grp = lax.axis_index("grp").astype(jnp.int32).reshape(1)
    z = lax.axis_index("z").astype(jnp.int32).reshape(1)
    dest = dest_group.reshape(1, -1)
    onward = [(i, i + 1) for i in range(NZ - 1)]
    backward = [(i + 1, i) for i in range(NZ - 1)]
    (kv_msg,) = call(
        settle_kv_kernel,
        [((32, 48, HD), BF)],
        (grp, dest, key_rows, value_rows, slot_segment),
        scalars=1,
    )
    (qg_msg,) = call(settle_qg_kernel, [((32, PAIR, HD), BF)], (dest, queries, out_grad))
    kv_got = exchange(kv_msg)
    own = call(arrange_kernel, [((2 * PAIR + 16, HD), BF)] * 2, (kv_got,), vm=VM_FEW)
    *own, qg_msg = lax.optimization_barrier((*own, qg_msg))
    qg_got = exchange(qg_msg)
    pairs = list(own)
    for _ in range(BACK):
        pairs = [lax.ppermute(x, "z", onward) for x in pairs[:2]] + pairs
    msg, *backs = attend(z, qg_got, *pairs)
    back = exchange(msg)
    moving = [lax.ppermute(x, "z", backward) for x in backs[:2]]
    for n in range(1, BACK):
        terms = backs[2 * n : 2 * n + 2]
        total = [(m.astype(F32) + t.astype(F32)).astype(BF) for m, t in zip(moving, terms)]
        moving = [lax.ppermute(x, "z", backward) for x in total]
    *moving, back = lax.optimization_barrier((*moving, back))
    (kv_back,) = call(kv_back_kernel, [((32, 64, HD), BF)], (*backs[-2:], *moving), vm=VM_FEW)
    kv_end = exchange(kv_back)
    rows = ((128, H * HD), BF)
    out, dq = call(unsettle_qg_kernel, [rows, rows], (dest, back), vm=VM_FEW)
    narrow = ((128, KV * HD), BF)
    dk, dv = call(unsettle_kv_kernel, [narrow, narrow], (grp, dest, kv_end), scalars=1, vm=VM_FEW)
    return out, dq, dk, dv


def solution(mesh):
    split = Mesh(mesh.devices.reshape(NG, NZ, NY), ("grp", "z", "y"))
    rows = P(("grp", "z", "y"), None)
    return jax.shard_map(
        on_device,
        mesh=split,
        in_specs=(rows, rows, rows, rows, rows, P("grp", ("z", "y"))),
        out_specs=(rows, rows, rows, rows),
        check_vma=False,
    )
```
